32 devices in a mesh: freq: 8 (over z, x), pair: 4 (over y, core).
Axes of the slice: x: 2, y: 2, z: 4, core: 2. Of those that a mesh axis runs over, the one named last changes fastest.
Arguments:
- voltages: int32 [2048, 103, 2048], P(('pair', 'freq')), may hold values from -8 to 7
- gains: float32 [2048, 24], P(('pair', 'freq')), may hold values from 0.3 to 3
Outputs:
- visibilities: bfloat16 [24, 2, 2048, 2048], P('freq', None, 'pair')
The draws below stay inside these ranges and needn't reach their ends.
All inputs are finite; a program needn't handle non-finite values.
Results may differ from the reference program's by a relative error of at most 0.0078.
Values may be sent and summed in bfloat16 or wider, within the bound.
No kernel may reach another device: no remote copies, remote signals or barrier semaphores. Data moves between devices by JAX's collectives and lax.ppermute only.
A program may use at most 192 MiB of HBM per device.

```python
import math
import jax
import jax.numpy as jnp
from jax import lax

INPUTS = 2048
NFFT = 2048
TAPS = 8
SAMPLES = 96
CHANNELS = 24
FRAMES = 103
FIRST = 256


def place_ends(array, stream_key, low, largest):
    shape = array.shape
    index_at = [jax.random.randint(jax.random.fold_in(stream_key, axis), (), 0, shape[axis]) for axis in range(len(shape))]
    array = array.at[tuple(index_at)].set(low)
    longest = shape.index(max(shape))
    index_at[longest] = (index_at[longest] + 1) % shape[longest]
    return array.at[tuple(index_at)].set(largest)


def levels(key, dims, shards, smallest, high):
    def one(position, shards_of):
        draws = jax.random.uniform(jax.random.fold_in(jax.random.fold_in(key, 6), position), (shards_of,), jnp.float32, smallest / len(shards), high / len(shards))
        return jnp.repeat(jnp.exp(draws), dims[position] // shards_of).reshape((-1,) + (1,) * (len(dims) - position - 1))

    loudness = one(*shards[0])
    for cut in shards[1:]:
        loudness = loudness * one(*cut)
    return loudness


def setup_inputs(seed: int = 0) -> dict:
    arg_keys = jax.random.split(jax.random.key(seed), 3)
    return {
        "voltages": place_ends(jax.random.randint(arg_keys[0], (INPUTS, FRAMES, NFFT), -8, 8), jax.random.fold_in(arg_keys[0], 1), -8, 7).astype(jnp.int32),
        "gains": jnp.clip(jnp.exp(math.log(3.0) - 2.3025851 * jax.random.uniform(arg_keys[1], (INPUTS, CHANNELS), jnp.float32) ** levels(arg_keys[1], (INPUTS, CHANNELS), ((0, 32),), -0.2, 0.2)), 0.3, 3.0),
    }


def filter_table():
    positions = jnp.arange(TAPS * NFFT, dtype=jnp.float32)
    span_width = float(TAPS * NFFT)
    window = 0.5 - 0.5 * jnp.cos(2.0 * jnp.pi * (positions + 0.5) / span_width)
    taps_table = window * jnp.sinc((positions - span_width / 2 + 0.5) / NFFT)
    return taps_table.reshape(TAPS, NFFT)

def dft_table(first_bin, count):
    samples = jnp.arange(NFFT, dtype=jnp.int32)
    bin_index = first_bin + jnp.arange(count, dtype=jnp.int32)
    phases = bin_index[:, None] * samples[None, :] % NFFT
    angles = phases.astype(jnp.float32) * (2.0 * math.pi / NFFT)
    amplitude = 0.25 / math.sqrt(NFFT)
    cos_rows = (jnp.cos(angles) * amplitude).astype(jnp.bfloat16)
    sin_rows = (-jnp.sin(angles) * amplitude).astype(jnp.bfloat16)
    return (cos_rows, sin_rows)

def reference(voltages, gains):
    taps_table = filter_table()
    cos_rows, sin_rows = dft_table(FIRST, CHANNELS)
    dft_rows = jnp.concatenate([cos_rows, sin_rows], 0).astype(jnp.float32)
    block_size = 64

    def channelize(parts):
        voltage_block, gain_block = parts
        as_float = voltage_block.astype(jnp.float32)
        filtered = taps_table[0] * as_float[:, 0:SAMPLES, :]
        for tap_index in range(1, TAPS):
            filtered = filtered + taps_table[tap_index] * as_float[:, tap_index:tap_index + SAMPLES, :]
        rounded = lax.optimization_barrier(filtered.astype(jnp.bfloat16))
        filtered = rounded.astype(jnp.float32)
        spectra = jnp.einsum('isn,kn->kis', filtered, dft_rows, precision=lax.Precision.HIGHEST)
        gain_rows = jnp.concatenate([gain_block.T, gain_block.T], 0)
        return (spectra * gain_rows[:, :, None]).astype(jnp.bfloat16)
    voltage_blocks = voltages.reshape(INPUTS // block_size, block_size, FRAMES, NFFT)
    gain_blocks = gains.reshape(INPUTS // block_size, block_size, CHANNELS)
    spectra = lax.map(channelize, (voltage_blocks, gain_blocks))
    spectra = spectra.transpose(1, 0, 2, 3).reshape(2, CHANNELS, INPUTS, SAMPLES)

    def correlate(parts):
        real_part = parts[0].astype(jnp.float32)
        imag_part = parts[1].astype(jnp.float32)

        def outer_product(left_side, right_side):
            return jnp.dot(left_side, right_side.T, precision=lax.Precision.HIGHEST)
        real_sum = outer_product(real_part, real_part) + outer_product(imag_part, imag_part)
        imag_sum = outer_product(imag_part, real_part) - outer_product(real_part, imag_part)
        return (jnp.stack([real_sum, imag_sum]) * (1.0 / SAMPLES)).astype(jnp.bfloat16)
    return lax.map(correlate, (spectra[0], spectra[1]))
```

```python
import functools
import math

import jax
import jax.numpy as jnp
import numpy as np
from jax import lax
from jax.experimental import pallas as pl
from jax.experimental.pallas import tpu as pltpu
from jax.sharding import PartitionSpec as P

NFFT = 2048
TAPS = 8
SAMPLES = 96
FIRST = 256
LANES = 128
VMEM_LIMIT = 36 * 1024 * 1024


def tables(channels):
    j = np.arange(TAPS * NFFT, dtype=np.float64)
    window = 0.5 - 0.5 * np.cos(2.0 * np.pi * (j + 0.5) / (TAPS * NFFT))
    taps = (window * np.sinc((j - TAPS * NFFT / 2 + 0.5) / NFFT)).astype(np.float32)
    bins = FIRST + np.arange(channels)
    angles = (bins[:, None] * np.arange(NFFT)[None, :] % NFFT) * (2.0 * math.pi / NFFT)
    amplitude = 0.25 / math.sqrt(NFFT)
    rows = np.stack([np.cos(angles) * amplitude, -np.sin(angles) * amplitude], 1)
    rows = rows.astype(np.float32).astype(jnp.bfloat16).astype(np.float32)
    return taps.reshape(TAPS, NFFT), rows.reshape(2 * channels, NFFT)


def channelize_kernel(rows, n_freq, x_hbm, tap_hbm, dft_hbm, gain_hbm, *refs):
    outs, refs = refs[:n_freq], refs[n_freq:]
    xs, ws, taps, dft, gains, carry, scale, sums, x_sem, sem = refs
    lanes = xs.shape[1]
    per_frame = lanes // TAPS
    tiles = lanes // LANES
    ahead = xs.shape[0] - 1
    piece = lanes // x_sem.shape[1]
    full, rest = divmod(x_hbm.shape[0], lanes)

    def copies(block, size):
        slot = lax.rem(block, xs.shape[0])
        found = []
        for k in range(x_sem.shape[1]):
            count = min(piece, size - k * piece)
            if count > 0:
                start = pl.multiple_of(block * lanes + k * piece, 16)
                found.append(
                    pltpu.make_async_copy(
                        x_hbm.at[pl.ds(start, count)],
                        xs.at[slot, pl.ds(k * piece, count)],
                        x_sem.at[slot, k],
                    )
                )
        return found

    def fetch(block):
        @pl.when(block < full)
        def _():
            for copy in copies(block, lanes):
                copy.start()

        if rest:

            @pl.when(block == full)
            def _():
                for copy in copies(block, rest):
                    copy.start()

    def block_of(block, size):
        for copy in copies(block, size):
            copy.wait()
        fetch(block + ahead)
        slot = lax.rem(block, xs.shape[0])
        part = min(256, lanes)
        pieces = []
        for at in range(0, lanes, part):
            x = xs[slot, at : at + part].astype(jnp.bfloat16)
            pieces.append(
                lax.dot_general(
                    ws[...], x, (((1,), (1,)), ((), ())), preferred_element_type=jnp.float32
                )
            )
        y = jnp.concatenate(pieces, axis=1)
        lane = lax.broadcasted_iota(jnp.int32, (rows, lanes), 1)
        low = y[0:rows]
        high = carry[...]
        for tap in range(1, TAPS):
            turned = pltpu.roll(y[tap * rows : (tap + 1) * rows], lanes - tap * per_frame, 1)
            keep = lane < lanes - tap * per_frame
            low = low + jnp.where(keep, turned, 0.0)
            high = high + jnp.where(keep, 0.0, turned)
        carry[...] = low
        for tile in range(tiles):
            sums[:, block * tiles + 8 - tiles + tile, :] = (
                high[:, tile * LANES : (tile + 1) * LANES] * scale[...]
            )

    small = [
        pltpu.make_async_copy(source, target, sem.at[k])
        for k, (source, target) in enumerate([(tap_hbm, taps), (dft_hbm, dft), (gain_hbm, gains)])
    ]
    for copy in small + copies(0, lanes):
        copy.start()
    row = lax.broadcasted_iota(jnp.int32, (rows, rows // 2), 0)
    column = lax.broadcasted_iota(jnp.int32, (rows, rows // 2), 1)
    spread = jnp.where(row // 2 == column, 1.0, 0.0).astype(jnp.float32)
    for copy in small:
        copy.wait()
    for tap in range(TAPS):
        ws[tap * rows : (tap + 1) * rows] = (taps[tap : tap + 1] * dft[...]).astype(jnp.bfloat16)
    for block in range(1, ahead):
        for copy in copies(block, lanes):
            copy.start()
    each = jnp.dot(
        spread,
        gains[...],
        precision=lax.Precision.HIGHEST,
        preferred_element_type=jnp.float32,
    )
    scale[...] = jnp.concatenate([each] * (LANES // per_frame), axis=1)
    carry[...] = jnp.zeros_like(carry)

    @pl.loop(0, full)
    def _(block):
        block_of(block, lanes)

    if rest:
        block_of(full, rest)
    share = rows // n_freq
    freq = lax.axis_index("freq")
    for k, out in enumerate(outs):
        block = sums[pl.ds((freq ^ k) * share, share), 8 : 8 + out.shape[2], :]
        out[0] = block.astype(jnp.bfloat16)


def channelize(x, taps, dft, gain, per_frame, n_freq):
    rows = dft.shape[0]
    lanes = TAPS * per_frame
    depth = SAMPLES // TAPS * (lanes // LANES)
    slots, pieces = 3, 4
    return pl.pallas_call(
        functools.partial(channelize_kernel, rows, n_freq),
        in_specs=[pl.BlockSpec(memory_space=pltpu.HBM)] * 4,
        out_specs=[pl.BlockSpec(memory_space=pltpu.VMEM)] * n_freq,
        out_shape=[jax.ShapeDtypeStruct((1, rows // n_freq, depth, LANES), jnp.bfloat16)] * n_freq,
        scratch_shapes=[
            pltpu.VMEM((slots, lanes, NFFT), jnp.int32),
            pltpu.VMEM((TAPS * rows, NFFT), jnp.bfloat16),
            pltpu.VMEM(taps.shape, jnp.float32),
            pltpu.VMEM(dft.shape, jnp.float32),
            pltpu.VMEM(gain.shape, jnp.float32),
            pltpu.VMEM((rows, lanes), jnp.float32),
            pltpu.VMEM((rows, LANES), jnp.float32),
            pltpu.VMEM((rows, depth + 8, LANES), jnp.float32),
            pltpu.SemaphoreType.DMA((slots, pieces)),
            pltpu.SemaphoreType.DMA((3,)),
        ],
        compiler_params=pltpu.CompilerParams(vmem_limit_bytes=VMEM_LIMIT),
        cost_estimate=pl.CostEstimate(
            flops=2 * x.shape[0] * NFFT * TAPS * rows,
            bytes_accessed=x.shape[0] * NFFT * 4,
            transcendentals=0,
        ),
        name="channelize",
    )(x, *[pltpu.with_memory_space_constraint(a, pltpu.HBM) for a in (taps, dft, gain)])


def columns(held, c, first, second, deep):
    half = LANES // 2
    rows = []
    for part in range(2):
        even, odd = held[first, c, part], held[second, c, part]
        rows.append(jnp.concatenate([even[:, :half], odd[:, :half]], axis=1))
        rows.append(jnp.concatenate([even[:, half:], odd[:, half:]], axis=1))
    used = sum(r.shape[0] for r in rows)
    if used < deep:
        rows.append(jnp.zeros((deep - used, LANES), rows[0].dtype))
    return jnp.concatenate(rows, axis=0)


def correlate_kernel(begins, blocks, *refs):
    if begins:
        refs, (out_hbm, lhs_ref, staged, sem) = refs[: len(blocks)], refs[len(blocks) :]
    else:
        lhs_ref, _, *refs, out_hbm, staged, sem = refs
    ch_dev, double, deep = lhs_ref.shape
    width = double // 2
    half = 2 * refs[0].shape[3]
    size = refs[0].shape[0]
    span = size // 2 * LANES
    freq, pair = lax.axis_index("freq"), lax.axis_index("pair")
    copies = []

    def tile(ref, group, c, k):
        flip = freq & (size - 1)
        return columns(ref, c, (2 * k) ^ flip, (2 * k + 1) ^ flip, deep)

    def place(group):
        return pl.multiple_of(((freq // size) ^ group) * span, span)

    for c in range(ch_dev):
        if begins:
            for ref, (slot, group) in zip(refs, blocks):
                if slot:
                    continue
                for k in range(size // 2):
                    own = tile(ref, group, c, k)
                    at = pl.multiple_of(place(group) + k * LANES, LANES)
                    lhs_ref[c, pl.ds(at, LANES), :] = own.T
                    swapped = [own[half : 2 * half], -own[0:half]]
                    if deep > 2 * half:
                        swapped.append(own[2 * half :])
                    swapped = jnp.concatenate(swapped, axis=0).T
                    lhs_ref[c, pl.ds(width + at, LANES), :] = swapped
        for n, (ref, (slot, group)) in enumerate(zip(refs, blocks)):
            rhs = jnp.concatenate([tile(ref, group, c, k) for k in range(size // 2)], axis=1)
            stage = staged.at[c * len(blocks) + n]
            for part in range(2):
                result = jnp.dot(
                    lhs_ref[c, part * width : (part + 1) * width],
                    rhs,
                    preferred_element_type=jnp.float32,
                )
                stage[part] = (result * (1.0 / SAMPLES)).astype(jnp.bfloat16)
            column = pl.multiple_of((pair ^ slot) * width + place(group), span)
            copy = pltpu.make_async_copy(
                stage, out_hbm.at[c, :, :, pl.ds(column, span)], sem.at[c * len(blocks) + n]
            )
            copy.start()
            copies.append(copy)
    for copy in copies:
        copy.wait()


def correlate(lhs, out, held, n_freq, n_pair, per_frame):
    blocks, arrays = list(held), list(held.values())
    _, ch_dev, _, depth, _ = arrays[0].shape
    width = n_freq * per_frame
    deep = -(-4 * depth // LANES) * LANES
    begins = lhs is None
    places = ch_dev * len(blocks)
    whole = pl.BlockSpec(memory_space=pltpu.VMEM)
    there = pl.BlockSpec(memory_space=pl.ANY)
    out_shape = jax.ShapeDtypeStruct((ch_dev, 2, width, n_pair * width), jnp.bfloat16)
    lhs_shape = jax.ShapeDtypeStruct((ch_dev, 2 * width, deep), jnp.bfloat16)
    first = [] if begins else [whole, there]
    return pl.pallas_call(
        functools.partial(correlate_kernel, begins, blocks),
        in_specs=first + [whole] * len(blocks),
        out_specs=[there, whole] if begins else there,
        out_shape=[out_shape, lhs_shape] if begins else out_shape,
        scratch_shapes=[
            pltpu.VMEM((places, 2, width, width // 2), jnp.bfloat16),
            pltpu.SemaphoreType.DMA((places,)),
        ],
        input_output_aliases={} if begins else {1: 0},
        compiler_params=pltpu.CompilerParams(vmem_limit_bytes=VMEM_LIMIT),
        cost_estimate=pl.CostEstimate(flops=0, bytes_accessed=0, transcendentals=0),
        name="correlate",
    )(*([] if begins else [lhs, out]), *arrays)


def correlate_plain(held, per_frame):
    freq, pair = lax.axis_index("freq"), lax.axis_index("pair")
    n_freq, n_pair = lax.axis_size("freq"), lax.axis_size("pair")
    size = n_freq // 2
    _, ch_dev, _, depth, _ = held[0, 0].shape
    share = LANES // per_frame
    order = jnp.arange(size) ^ (freq & (size - 1))
    sides = [jnp.stack([held[slot, 0][order], held[slot, 1][order]]) for slot in range(n_pair)]
    blocks = jnp.stack(sides)[jnp.arange(n_pair) ^ pair][:, jnp.arange(2) ^ (freq // size)]

    def matrix(array):
        array = array.reshape(-1, n_freq, ch_dev, 2, depth, share, per_frame)
        return array.transpose(2, 3, 4, 5, 0, 1, 6).reshape(ch_dev, 2, depth * share, -1)

    row, col = matrix(lax.dynamic_index_in_dim(blocks, pair, 0)), matrix(blocks)

    def contract(a, b):
        return jnp.einsum("csr,csk->crk", a, b, preferred_element_type=jnp.float32)

    real = contract(row[:, 0], col[:, 0]) + contract(row[:, 1], col[:, 1])
    imag = contract(row[:, 1], col[:, 0]) - contract(row[:, 0], col[:, 1])
    return (jnp.stack([real, imag], axis=1) * (1.0 / SAMPLES)).astype(jnp.bfloat16)


def exchange(array, mask):
    size = lax.axis_size("pair")
    return lax.ppermute(array, "pair", [(i, i ^ mask) for i in range(size)])


def body(voltages, gains):
    n_freq, n_pair = lax.axis_size("freq"), lax.axis_size("pair")
    per_frame, frames, _ = voltages.shape
    channels = gains.shape[1]
    ch_dev, size = channels // n_freq, n_freq // 2
    taps, dft = [jnp.asarray(table) for table in tables(channels)]
    x = voltages.transpose(1, 0, 2).reshape(frames * per_frame, NFFT)
    spectra = channelize(x, taps, dft, gains.T, per_frame, n_freq)
    spectra = [a.reshape(1, ch_dev, 2, -1, LANES) for a in spectra]
    spectra = spectra[:1] + [
        lax.ppermute(a, "freq", [(f, f ^ k) for f in range(n_freq)])
        for k, a in enumerate(spectra)
        if k
    ]
    first = jnp.concatenate(spectra[: size // 2])
    second = jnp.concatenate(spectra[size // 2 : size + 1])
    near, far = jnp.concatenate(spectra[:size]), spectra[size:]
    across = [exchange(first, 2), exchange(second, 2)]
    far[1:], across[0] = lax.optimization_barrier((far[1:], across[0]))
    last = exchange(jnp.concatenate(far[1:]), 2)
    far = jnp.concatenate(far)
    held = {(0, 0): near, (1, 0): exchange(near, 1), (0, 1): far, (1, 1): exchange(far, 1)}
    held[2, 0] = jnp.concatenate([across[0], across[1][: size // 2]])
    held[3, 0] = exchange(held[2, 0], 1)
    early = across[1][size // 2 :]
    if n_freq != 8 or 2 * per_frame != LANES or near.shape[3] % 16:
        held[2, 1] = jnp.concatenate([early, last])
        held[3, 1] = exchange(held[2, 1], 1)
        return correlate_plain(held, per_frame)

    def part(lhs, out, *which):
        return correlate(lhs, out, {w: held[w] for w in which}, n_freq, n_pair, per_frame)

    out, lhs = part(None, None, (0, 0), (0, 1), (1, 0), (2, 0), (3, 0), (1, 1))
    last, out = lax.optimization_barrier((last, out))
    held[2, 1] = jnp.concatenate([early, last])
    held[3, 1] = exchange(held[2, 1], 1)
    return part(lhs, out, (2, 1), (3, 1))


def solution(mesh):
    placed = (P(("pair", "freq"), None, None), P(("pair", "freq"), None))
    return jax.shard_map(
        body, mesh=mesh, in_specs=placed, out_specs=P("freq", None, "pair", None), check_vma=False
    )
```

```python
import functools
import math

import jax
import jax.numpy as jnp
import numpy as np
from jax import lax
from jax.experimental import pallas as pl
from jax.experimental.pallas import tpu as pltpu
from jax.sharding import PartitionSpec as P

NFFT = 2048
TAPS = 8
SAMPLES = 96
FIRST = 256
LANES = 128
VMEM_LIMIT = 36 * 1024 * 1024


def tables(channels):
    j = np.arange(TAPS * NFFT, dtype=np.float64)
    window = 0.5 - 0.5 * np.cos(2.0 * np.pi * (j + 0.5) / (TAPS * NFFT))
    taps = (window * np.sinc((j - TAPS * NFFT / 2 + 0.5) / NFFT)).astype(np.float32)
    bins = FIRST + np.arange(channels)
    angles = (bins[:, None] * np.arange(NFFT)[None, :] % NFFT) * (2.0 * math.pi / NFFT)
    amplitude = 0.25 / math.sqrt(NFFT)
    rows = np.stack([np.cos(angles) * amplitude, -np.sin(angles) * amplitude], 1)
    rows = rows.astype(np.float32).astype(jnp.bfloat16).astype(np.float32)
    return taps.reshape(TAPS, NFFT), rows.reshape(2 * channels, NFFT)


def channelize_kernel(rows, n_freq, x_hbm, tap_hbm, dft_hbm, gain_hbm, *refs):
    outs, refs = refs[:n_freq], refs[n_freq:]
    xs, ws, taps, dft, gains, carry, scale, sums, x_sem, sem = refs
    lanes = xs.shape[1]
    per_frame = lanes // TAPS
    tiles = lanes // LANES
    ahead = xs.shape[0] - 1
    piece = lanes // x_sem.shape[1]
    full, rest = divmod(x_hbm.shape[0], lanes)

    def copies(block, size):
        slot = lax.rem(block, xs.shape[0])
        found = []
        for k in range(x_sem.shape[1]):
            count = min(piece, size - k * piece)
            if count > 0:
                start = pl.multiple_of(block * lanes + k * piece, 16)
                found.append(
                    pltpu.make_async_copy(
                        x_hbm.at[pl.ds(start, count)],
                        xs.at[slot, pl.ds(k * piece, count)],
                        x_sem.at[slot, k],
                    )
                )
        return found

    def fetch(block):
        @pl.when(block < full)
        def _():
            for copy in copies(block, lanes):
                copy.start()

        if rest:

            @pl.when(block == full)
            def _():
                for copy in copies(block, rest):
                    copy.start()

    def block_of(block, size):
        for copy in copies(block, size):
            copy.wait()
        fetch(block + ahead)
        slot = lax.rem(block, xs.shape[0])
        part = min(256, lanes)
        pieces = []
        for at in range(0, lanes, part):
            x = xs[slot, at : at + part].astype(jnp.bfloat16)
            pieces.append(
                lax.dot_general(
                    ws[...], x, (((1,), (1,)), ((), ())), preferred_element_type=jnp.float32
                )
            )
        y = jnp.concatenate(pieces, axis=1)
        lane = lax.broadcasted_iota(jnp.int32, (rows, lanes), 1)
        low = y[0:rows]
        high = carry[...]
        for tap in range(1, TAPS):
            turned = pltpu.roll(y[tap * rows : (tap + 1) * rows], lanes - tap * per_frame, 1)
            keep = lane < lanes - tap * per_frame
            low = low + jnp.where(keep, turned, 0.0)
            high = high + jnp.where(keep, 0.0, turned)
        carry[...] = low
        for tile in range(tiles):
            sums[:, block * tiles + 8 - tiles + tile, :] = (
                high[:, tile * LANES : (tile + 1) * LANES] * scale[...]
            )

    small = [
        pltpu.make_async_copy(source, target, sem.at[k])
        for k, (source, target) in enumerate([(tap_hbm, taps), (dft_hbm, dft), (gain_hbm, gains)])
    ]
    for copy in small + copies(0, lanes):
        copy.start()
    row = lax.broadcasted_iota(jnp.int32, (rows, rows // 2), 0)
    column = lax.broadcasted_iota(jnp.int32, (rows, rows // 2), 1)
    spread = jnp.where(row // 2 == column, 1.0, 0.0).astype(jnp.float32)
    for copy in small:
        copy.wait()
    for tap in range(TAPS):
        ws[tap * rows : (tap + 1) * rows] = (taps[tap : tap + 1] * dft[...]).astype(jnp.bfloat16)
    for block in range(1, ahead):
        for copy in copies(block, lanes):
            copy.start()
    each = jnp.dot(
        spread,
        gains[...],
        precision=lax.Precision.HIGHEST,
        preferred_element_type=jnp.float32,
    )
    scale[...] = jnp.concatenate([each] * (LANES // per_frame), axis=1)
    carry[...] = jnp.zeros_like(carry)

    @pl.loop(0, full)
    def _(block):
        block_of(block, lanes)

    if rest:
        block_of(full, rest)
    share = rows // n_freq
    freq = lax.axis_index("freq")
    for k, out in enumerate(outs):
        block = sums[pl.ds((freq ^ k) * share, share), 8 : 8 + out.shape[2], :]
        out[0] = block.astype(jnp.bfloat16)


def channelize(x, taps, dft, gain, per_frame, n_freq):
    rows = dft.shape[0]
    lanes = TAPS * per_frame
    depth = SAMPLES // TAPS * (lanes // LANES)
    slots, pieces = 3, 4
    return pl.pallas_call(
        functools.partial(channelize_kernel, rows, n_freq),
        in_specs=[pl.BlockSpec(memory_space=pltpu.HBM)] * 4,
        out_specs=[pl.BlockSpec(memory_space=pltpu.VMEM)] * n_freq,
        out_shape=[jax.ShapeDtypeStruct((1, rows // n_freq, depth, LANES), jnp.bfloat16)] * n_freq,
        scratch_shapes=[
            pltpu.VMEM((slots, lanes, NFFT), jnp.int32),
            pltpu.VMEM((TAPS * rows, NFFT), jnp.bfloat16),
            pltpu.VMEM(taps.shape, jnp.float32),
            pltpu.VMEM(dft.shape, jnp.float32),
            pltpu.VMEM(gain.shape, jnp.float32),
            pltpu.VMEM((rows, lanes), jnp.float32),
            pltpu.VMEM((rows, LANES), jnp.float32),
            pltpu.VMEM((rows, depth + 8, LANES), jnp.float32),
            pltpu.SemaphoreType.DMA((slots, pieces)),
            pltpu.SemaphoreType.DMA((3,)),
        ],
        compiler_params=pltpu.CompilerParams(vmem_limit_bytes=VMEM_LIMIT),
        cost_estimate=pl.CostEstimate(
            flops=2 * x.shape[0] * NFFT * TAPS * rows,
            bytes_accessed=x.shape[0] * NFFT * 4,
            transcendentals=0,
        ),
        name="channelize",
    )(x, *[pltpu.with_memory_space_constraint(a, pltpu.HBM) for a in (taps, dft, gain)])


def columns(held, c, first, second, deep):
    half = LANES // 2
    rows = []
    for part in range(2):
        even, odd = held[first, c, part], held[second, c, part]
        rows.append(jnp.concatenate([even[:, :half], odd[:, :half]], axis=1))
        rows.append(jnp.concatenate([even[:, half:], odd[:, half:]], axis=1))
    used = sum(r.shape[0] for r in rows)
    if used < deep:
        rows.append(jnp.zeros((deep - used, LANES), rows[0].dtype))
    return jnp.concatenate(rows, axis=0)


def correlate_kernel(begins, blocks, *refs):
    if begins:
        refs, (out_hbm, lhs_ref, staged, sem) = refs[: len(blocks)], refs[len(blocks) :]
    else:
        lhs_ref, _, *refs, out_hbm, staged, sem = refs
    ch_dev, double, deep = lhs_ref.shape
    width = double // 2
    half = 2 * refs[0].shape[3]
    size = refs[0].shape[0]
    span = size // 2 * LANES
    freq, pair = lax.axis_index("freq"), lax.axis_index("pair")
    copies = []

    def tile(ref, group, c, k):
        flip = freq & (size - 1)
        return columns(ref, c, (2 * k) ^ flip, (2 * k + 1) ^ flip, deep)

    def place(group):
        return pl.multiple_of(((freq // size) ^ group) * span, span)

    for c in range(ch_dev):
        if begins:
            for ref, (slot, group) in zip(refs, blocks):
                if slot:
                    continue
                for k in range(size // 2):
                    own = tile(ref, group, c, k)
                    at = pl.multiple_of(place(group) + k * LANES, LANES)
                    lhs_ref[c, pl.ds(at, LANES), :] = own.T
                    swapped = [own[half : 2 * half], -own[0:half]]
                    if deep > 2 * half:
                        swapped.append(own[2 * half :])
                    swapped = jnp.concatenate(swapped, axis=0).T
                    lhs_ref[c, pl.ds(width + at, LANES), :] = swapped
        for n, (ref, (slot, group)) in enumerate(zip(refs, blocks)):
            rhs = jnp.concatenate([tile(ref, group, c, k) for k in range(size // 2)], axis=1)
            stage = staged.at[c * len(blocks) + n]
            for part in range(2):
                result = jnp.dot(
                    lhs_ref[c, part * width : (part + 1) * width],
                    rhs,
                    preferred_element_type=jnp.float32,
                )
                stage[part] = (result * (1.0 / SAMPLES)).astype(jnp.bfloat16)
            column = pl.multiple_of((pair ^ slot) * width + place(group), span)
            copy = pltpu.make_async_copy(
                stage, out_hbm.at[c, :, :, pl.ds(column, span)], sem.at[c * len(blocks) + n]
            )
            copy.start()
            copies.append(copy)
    for copy in copies:
        copy.wait()


def correlate(lhs, out, held, n_freq, n_pair, per_frame):
    blocks, arrays = list(held), list(held.values())
    _, ch_dev, _, depth, _ = arrays[0].shape
    width = n_freq * per_frame
    deep = -(-4 * depth // LANES) * LANES
    begins = lhs is None
    places = ch_dev * len(blocks)
    whole = pl.BlockSpec(memory_space=pltpu.VMEM)
    there = pl.BlockSpec(memory_space=pl.ANY)
    out_shape = jax.ShapeDtypeStruct((ch_dev, 2, width, n_pair * width), jnp.bfloat16)
    lhs_shape = jax.ShapeDtypeStruct((ch_dev, 2 * width, deep), jnp.bfloat16)
    first = [] if begins else [whole, there]
    return pl.pallas_call(
        functools.partial(correlate_kernel, begins, blocks),
        in_specs=first + [whole] * len(blocks),
        out_specs=[there, whole] if begins else there,
        out_shape=[out_shape, lhs_shape] if begins else out_shape,
        scratch_shapes=[
            pltpu.VMEM((places, 2, width, width // 2), jnp.bfloat16),
            pltpu.SemaphoreType.DMA((places,)),
        ],
        input_output_aliases={} if begins else {1: 0},
        compiler_params=pltpu.CompilerParams(vmem_limit_bytes=VMEM_LIMIT),
        cost_estimate=pl.CostEstimate(flops=0, bytes_accessed=0, transcendentals=0),
        name="correlate",
    )(*([] if begins else [lhs, out]), *arrays)


def correlate_plain(held, per_frame):
    freq, pair = lax.axis_index("freq"), lax.axis_index("pair")
    n_freq, n_pair = lax.axis_size("freq"), lax.axis_size("pair")
    size = n_freq // 2
    _, ch_dev, _, depth, _ = held[0, 0].shape
    share = LANES // per_frame
    order = jnp.arange(size) ^ (freq & (size - 1))
    sides = [jnp.stack([held[slot, 0][order], held[slot, 1][order]]) for slot in range(n_pair)]
    blocks = jnp.stack(sides)[jnp.arange(n_pair) ^ pair][:, jnp.arange(2) ^ (freq // size)]

    def matrix(array):
        array = array.reshape(-1, n_freq, ch_dev, 2, depth, share, per_frame)
        return array.transpose(2, 3, 4, 5, 0, 1, 6).reshape(ch_dev, 2, depth * share, -1)

    row, col = matrix(lax.dynamic_index_in_dim(blocks, pair, 0)), matrix(blocks)

    def contract(a, b):
        return jnp.einsum("csr,csk->crk", a, b, preferred_element_type=jnp.float32)

    real = contract(row[:, 0], col[:, 0]) + contract(row[:, 1], col[:, 1])
    imag = contract(row[:, 1], col[:, 0]) - contract(row[:, 0], col[:, 1])
    return (jnp.stack([real, imag], axis=1) * (1.0 / SAMPLES)).astype(jnp.bfloat16)


def exchange(array, mask):
    size = lax.axis_size("pair")
    return lax.ppermute(array, "pair", [(i, i ^ mask) for i in range(size)])


def body(voltages, gains):
    n_freq, n_pair = lax.axis_size("freq"), lax.axis_size("pair")
    per_frame, frames, _ = voltages.shape
    channels = gains.shape[1]
    ch_dev, size = channels // n_freq, n_freq // 2
    taps, dft = [jnp.asarray(table) for table in tables(channels)]
    x = voltages.transpose(1, 0, 2).reshape(frames * per_frame, NFFT)
    spectra = channelize(x, taps, dft, gains.T, per_frame, n_freq)
    spectra = [a.reshape(1, ch_dev, 2, -1, LANES) for a in spectra]
    spectra = spectra[:1] + [
        lax.ppermute(a, "freq", [(f, f ^ k) for f in range(n_freq)])
        for k, a in enumerate(spectra)
        if k
    ]
    first = jnp.concatenate(spectra[: size // 2])
    second = jnp.concatenate(spectra[size // 2 : size + 1])
    near, far = jnp.concatenate(spectra[:size]), spectra[size:]
    across = [exchange(first, 2), exchange(second, 2)]
    far[1:], across[0] = lax.optimization_barrier((far[1:], across[0]))
    last = exchange(jnp.concatenate(far[1:]), 2)
    far = jnp.concatenate(far)
    held = {(0, 0): near, (1, 0): exchange(near, 1), (0, 1): far, (1, 1): exchange(far, 1)}
    held[2, 0] = jnp.concatenate([across[0], across[1][: size // 2]])
    held[3, 0] = exchange(held[2, 0], 1)
    early = across[1][size // 2 :]
    if n_freq != 8 or 2 * per_frame != LANES or near.shape[3] % 16:
        held[2, 1] = jnp.concatenate([early, last])
        held[3, 1] = exchange(held[2, 1], 1)
        return correlate_plain(held, per_frame)

    def part(lhs, out, *which):
        return correlate(lhs, out, {w: held[w] for w in which}, n_freq, n_pair, per_frame)

    out, lhs = part(None, None, (0, 0), (0, 1), (1, 0), (1, 1))
    last, out = lax.optimization_barrier((last, out))
    held[2, 1] = jnp.concatenate([early, last])
    held[3, 1] = exchange(held[2, 1], 1)
    out = part(lhs, out, (2, 0), (3, 0))
    return part(lhs, out, (2, 1), (3, 1))


def solution(mesh):
    placed = (P(("pair", "freq"), None, None), P(("pair", "freq"), None))
    return jax.shard_map(
        body, mesh=mesh, in_specs=placed, out_specs=P("freq", None, "pair", None), check_vma=False
    )
```
